32 devices in a mesh: user: 16 (over z, y, x), item: 2 (over core).
Axes of the slice: x: 2, y: 2, z: 4, core: 2. Of those that a mesh axis runs over, the one named last changes fastest.
Arguments:
- user_factors: bfloat16 [16384, 256], P('user'), may hold values from -0.3984375 to 0.3984375
- item_panels: float32 [32768, 256], P(('user', 'item')), may hold values from -6 to 6
- ratings: bfloat16 [3, 384, 256, 128], P(None, 'user', 'item'), may hold values from -6 to 6
- tile_ids: int32 [3, 384, 2], P(None, 'user', 'item'), may hold values from 0 to 63, as said below
- tile_count: int32 [3, 16, 2], P(None, 'user', 'item'), may hold values from 6 to 24, as said below
Outputs:
- panels_out: float32 [32768, 256], P(('user', 'item'))
- user_grad: float32 [16384, 256], P(('user', 'item'))
The draws below stay inside these ranges and needn't reach their ends.
Inputs may be any that keep to these rules, and one draw needn't show every extreme that they name: `tile_ids`: the first 24 entries of each user block's list for a group and step are distinct tiles of the block. `tile_count`: in every step some user block and group has all 24 slots live.
All inputs are finite; a program needn't handle non-finite values.
Results may differ from the reference program's by a relative error of at most 0.0013.
Values sent between devices are 32-bit elements; how exact they have to be, the bound alone decides.
A program may use at most 64 MiB of HBM per device.

```python
import jax
import jax.numpy as jnp
from jax import lax

R = 256
TILE = 128
USER_ROWS = 1024
PANEL = 1024
STEPS = 3
TILES_BLOCK = 64
SLOTS = 24
CYCLE = 16
GROUPS = 2
USERS = 16384
ITEMS = 32768
SLOT_ROWS = 384
GROUP_ROWS = 256


def draw_tile_ids(key, part):
    keys = jax.random.split(jax.random.fold_in(key, 11), STEPS * CYCLE * GROUPS)
    chosen = jax.vmap(lambda one_key: jax.random.permutation(one_key, TILES_BLOCK)[:SLOTS])(keys)
    chosen = chosen.reshape(STEPS, CYCLE, GROUPS, SLOTS).transpose(0, 1, 3, 2)
    return chosen.reshape(STEPS, CYCLE * SLOTS, GROUPS).astype(jnp.int32)


def draw_tile_count(key, part):
    base = jax.random.randint(jax.random.fold_in(key, 21), (STEPS, CYCLE * GROUPS), (SLOTS + 3) // 4, SLOTS + 1)
    fullest = jax.random.randint(jax.random.fold_in(key, 22), (STEPS, 1), 0, CYCLE * GROUPS)
    places = jnp.arange(CYCLE * GROUPS)[None, :]
    counts = jnp.where(places == fullest, SLOTS, base)
    return counts.reshape(STEPS, CYCLE, GROUPS).astype(jnp.int32)


def block_levels(own_key, shape, cuts, least, top_value):
    loudness = 1.0
    for position, blocks in cuts:
        heights = jax.random.uniform(jax.random.fold_in(jax.random.fold_in(own_key, 6), position), (blocks,), jnp.float32, least / len(cuts), top_value / len(cuts))
        loudness = loudness * jnp.repeat(jnp.exp(heights), shape[position] // blocks).reshape((-1,) + (1,) * (len(shape) - 1 - position))
    return loudness


def normal_values(own_key, extent, deviation, reach, shards=(), held_as=jnp.bfloat16):
    factor_of = block_levels(own_key, extent, shards, -0.22, 0.18) if shards else 1.0
    result = jax.random.normal(own_key, extent, jnp.float32) * deviation * factor_of
    return jnp.minimum(jnp.maximum(result, -reach), reach).astype(held_as)


def setup_inputs(seed: int = 0) -> dict:
    splits = jax.random.split(jax.random.key(seed), 6)
    return {
        "user_factors": normal_values(splits[0], (USERS, R), 0.0625, 0.3984375, ((0, 16),)),
        "item_panels": normal_values(splits[1], (ITEMS, R), 1.0, 6.0, ((0, 32),), jnp.float32),
        "ratings": normal_values(splits[2], (STEPS, SLOT_ROWS, GROUP_ROWS, TILE), 1.0, 6.0, ((1, 16), (2, 2))),
        "tile_ids": draw_tile_ids(jax.random.fold_in(splits[5], 71), 0),
        "tile_count": draw_tile_count(jax.random.fold_in(splits[5], 71), 0),
    }


learn_rate = 0.05
weight_decay = 0.02
user_scale = 1.0 / 64.0


def update_block(user_block, item_block, rating_tiles, tile_list, live_count):
    row_tiles = user_block.shape[0] // TILE
    col_tiles = item_block.shape[0] // TILE
    row_index = tile_list // col_tiles
    col_index = tile_list % col_tiles
    user_tiles = user_block.astype(jnp.float32).reshape(row_tiles, TILE, R)[row_index]
    item_tiles = item_block.astype(jnp.bfloat16).astype(jnp.float32).reshape(col_tiles, TILE, R)[col_index]
    predicted = jnp.einsum("kir,kjr->kij", user_tiles, item_tiles, precision=lax.Precision.HIGHEST)
    live_mask = (jnp.arange(tile_list.shape[0]) < live_count).astype(jnp.float32)
    residual = ((predicted - rating_tiles.astype(jnp.float32)) * live_mask[:, None, None]).astype(jnp.bfloat16).astype(jnp.float32)
    item_parts = jnp.einsum("kij,kir->kjr", residual, user_tiles, precision=lax.Precision.HIGHEST)
    user_parts = jnp.einsum("kij,kjr->kir", residual, item_tiles, precision=lax.Precision.HIGHEST)
    col_pick = (col_index[:, None] == jnp.arange(col_tiles)[None, :]).astype(jnp.float32)
    row_pick = (row_index[:, None] == jnp.arange(row_tiles)[None, :]).astype(jnp.float32)
    item_grad = jnp.einsum("kc,kjr->cjr", col_pick, item_parts, precision=lax.Precision.HIGHEST).reshape(-1, R)
    user_grad = jnp.einsum("ka,kir->air", row_pick, user_parts, precision=lax.Precision.HIGHEST).reshape(-1, R)
    new_block = item_block - learn_rate * (item_grad + weight_decay * item_block)
    return new_block, user_scale * user_grad


def reference(user_factors, item_panels, ratings, tile_ids, tile_count):
    user_blocks = user_factors.reshape(CYCLE, USER_ROWS, R)
    panels = item_panels.reshape(CYCLE, GROUPS, PANEL, R)
    rating_all = ratings.reshape(STEPS, CYCLE, SLOTS, GROUPS, TILE, TILE)
    list_all = tile_ids.reshape(STEPS, CYCLE, SLOTS, GROUPS)
    gradient = jnp.zeros((CYCLE, USER_ROWS, R), jnp.float32)

    def per_user(packed):
        user_block, group_panels, group_ratings, group_lists, group_counts = packed
        new_panels, user_parts = jax.vmap(update_block, in_axes=(None, 0, 1, 1, 0))(
            user_block, group_panels, group_ratings, group_lists, group_counts)
        return new_panels, jnp.sum(user_parts, axis=0)

    for step_index in range(STEPS):
        if step_index > 0:
            panels = jnp.roll(panels, 1, axis=0)
        panels, user_parts = lax.map(per_user, (user_blocks, panels, rating_all[step_index],
                                                list_all[step_index], tile_count[step_index]))
        gradient = gradient + user_parts
    return panels.reshape(ITEMS, R), gradient.reshape(USERS, R)
```

```python
import functools

import jax
import jax.numpy as jnp
from jax import lax
from jax.experimental import pallas as pl
from jax.experimental.pallas import tpu as pltpu
from jax.sharding import PartitionSpec as P

TILE = 128
CHUNK = 256
MESH = pl.DeviceIdType.MESH

learn_rate = 0.05
weight_decay = 0.02
user_scale = 1.0 / 64.0


def kernel(
    steps, cycle, groups,
    slot_ref, users_hbm, panel_hbm, ratings_hbm, panel_out, grad_out,
    users, total, residual, grad_in, held, ratings,
    load_sem, rate_sem, send_sem, recv_sem, out_sem, grad_send, grad_recv,
):
    rows, rank = users.shape
    items = held[0].shape[0]
    slots = ratings[0].shape[0]
    row_tiles, col_tiles = rows // TILE, items // TILE
    chunks = items // CHUNK
    wide = CHUNK // TILE
    share = rows // groups

    u = lax.axis_index("user")
    g = lax.axis_index("item")
    right, left = lax.rem(u + 1, cycle), lax.rem(u + cycle - 1, cycle)

    barrier = pltpu.get_barrier_semaphore()
    for neighbour in (left, right):
        pl.semaphore_signal(barrier, inc=1, device_id={"user": neighbour}, device_id_type=MESH)
    for d in range(1, groups):
        pl.semaphore_signal(
            barrier, inc=1, device_id={"item": lax.rem(g + d, groups)}, device_id_type=MESH
        )

    def part(c):
        return pl.ds(pl.multiple_of(c * CHUNK, CHUNK), CHUNK)

    load_users = pltpu.make_async_copy(users_hbm, users, load_sem.at[chunks])
    load_panel = [
        pltpu.make_async_copy(panel_hbm.at[part(c)], held[0].at[part(c)], load_sem.at[c])
        for c in range(chunks)
    ]
    load_rates = [
        pltpu.make_async_copy(ratings_hbm.at[s], ratings[s], rate_sem.at[s]) for s in range(steps)
    ]
    load_panel[0].start()
    load_users.start()
    load_rates[0].start()
    for c in range(1, chunks):
        load_panel[c].start()
    for s in range(1, steps):
        load_rates[s].start()

    def send(s, c):
        return pltpu.make_async_remote_copy(
            src_ref=held[s].at[part(c)],
            dst_ref=held[s + 1].at[part(c)],
            send_sem=send_sem.at[s, c],
            recv_sem=recv_sem.at[s, c],
            device_id={"user": right},
            device_id_type=MESH,
        )

    def write(c):
        return pltpu.make_async_copy(held[-1].at[part(c)], panel_out.at[part(c)], out_sem.at[c])

    def update(s, c):
        panel = held[s][part(c), :]
        rounded = panel.astype(jnp.bfloat16)
        for top in range(0, rows, CHUNK):
            predicted = lax.dot_general(
                users[top : top + CHUNK, :], rounded, (((1,), (1,)), ((), ())),
                preferred_element_type=jnp.float32,
            )
            for i in range(wide):
                for j in range(wide):
                    slot = slot_ref[s, (top // TILE + i) * col_tiles + c * wide + j]
                    live = (slot < slots).astype(jnp.float32)
                    rated = ratings[s][jnp.minimum(slot, slots - 1)].astype(jnp.float32)
                    guess = predicted[i * TILE : (i + 1) * TILE, j * TILE : (j + 1) * TILE]
                    residual[
                        top + i * TILE : top + (i + 1) * TILE, j * TILE : (j + 1) * TILE
                    ] = ((guess - rated) * live).astype(jnp.bfloat16)
        item_grad = lax.dot_general(
            residual[...], users[...], (((0,), (0,)), ((), ())),
            preferred_element_type=jnp.float32,
        )
        held[s][part(c), :] = panel - learn_rate * (item_grad + weight_decay * panel)
        return rounded

    def add_users(rounded):
        for top in range(0, rows, CHUNK):
            total[top : top + CHUNK, :] += jnp.dot(
                residual[top : top + CHUNK, :], rounded, preferred_element_type=jnp.float32
            )

    total[...] = jnp.zeros_like(total)
    load_users.wait()
    for s in range(steps):
        load_rates[s].wait()

        def work(c, carry, s=s):
            if s == 0:
                pltpu.make_async_copy(
                    panel_hbm.at[part(c)], held[0].at[part(c)], load_sem.at[c]
                ).wait()
            else:
                send(s - 1, c).wait_recv()
            rounded = update(s, c)
            if s == 0:
                @pl.when(c == 0)
                def _():
                    pl.semaphore_wait(barrier, 2 + groups - 1)
            if s < steps - 1:
                send(s, c).start()
            else:
                write(c).start()
            add_users(rounded)
            return carry

        lax.fori_loop(0, chunks, work, 0)

    def exchange(d):
        peer = lax.rem(g + d, groups)
        return pltpu.make_async_remote_copy(
            src_ref=total.at[pl.ds(pl.multiple_of(peer * share, share), share)],
            dst_ref=grad_in.at[d - 1],
            send_sem=grad_send.at[d - 1],
            recv_sem=grad_recv.at[d - 1],
            device_id={"item": peer},
            device_id_type=MESH,
        )

    for d in range(1, groups):
        exchange(d).start()
    mine = pl.ds(pl.multiple_of(g * share, share), share)
    for d in range(1, groups):
        exchange(d).wait_recv()
        total[mine, :] += grad_in[d - 1]
    total[mine, :] = user_scale * total[mine, :]
    finish = pltpu.make_async_copy(total.at[mine], grad_out, load_sem.at[chunks])
    finish.start()
    for d in range(1, groups):
        exchange(d).wait_send()
    for s in range(steps - 1):
        for c in range(chunks):
            send(s, c).wait_send()
    for c in range(chunks):
        write(c).wait()
    finish.wait()


def shards(user_factors, item_panels, ratings, tile_ids, tile_count):
    cycle, groups = lax.axis_size("user"), lax.axis_size("item")
    rows, rank = user_factors.shape
    items = item_panels.shape[0]
    steps, slots = ratings.shape[:2]
    chunks = items // CHUNK
    tiles = (rows // TILE) * (items // TILE)
    share = rows // groups

    order = jnp.arange(slots, dtype=jnp.int32)[None, :, None]
    listed = (tile_ids == jnp.arange(tiles, dtype=jnp.int32)) & (order < tile_count)
    slot_of = jnp.min(jnp.where(listed, order, slots), axis=1)

    anywhere = pl.BlockSpec(memory_space=pl.ANY)
    return pl.pallas_call(
        functools.partial(kernel, steps, cycle, groups),
        out_shape=(
            jax.ShapeDtypeStruct((items, rank), jnp.float32),
            jax.ShapeDtypeStruct((share, rank), jnp.float32),
        ),
        in_specs=[pl.BlockSpec(memory_space=pltpu.SMEM)] + [anywhere] * 3,
        out_specs=(anywhere, anywhere),
        scratch_shapes=[
            pltpu.VMEM((rows, rank), jnp.bfloat16),
            pltpu.VMEM((rows, rank), jnp.float32),
            pltpu.VMEM((rows, CHUNK), jnp.bfloat16),
            pltpu.VMEM((max(groups - 1, 1), share, rank), jnp.float32),
            [pltpu.VMEM((items, rank), jnp.float32) for _ in range(steps)],
            [pltpu.VMEM((slots, TILE, TILE), jnp.bfloat16) for _ in range(steps)],
            pltpu.SemaphoreType.DMA((chunks + 1,)),
            pltpu.SemaphoreType.DMA((steps,)),
            pltpu.SemaphoreType.DMA((steps - 1, chunks)),
            pltpu.SemaphoreType.DMA((steps - 1, chunks)),
            pltpu.SemaphoreType.DMA((chunks,)),
            pltpu.SemaphoreType.DMA((max(groups - 1, 1),)),
            pltpu.SemaphoreType.DMA((max(groups - 1, 1),)),
        ],
        compiler_params=pltpu.CompilerParams(
            collective_id=0, has_side_effects=True, vmem_limit_bytes=32 * 2**20
        ),
        name="sub_epoch",
    )(slot_of, user_factors, item_panels, ratings)


def solution(mesh):
    in_specs = (
        P("user", None),
        P(("user", "item"), None),
        P(None, "user", "item", None),
        P(None, "user", "item"),
        P(None, "user", "item"),
    )
    out_specs = (P(("user", "item"), None), P(("user", "item"), None))
    return jax.shard_map(shards, mesh=mesh, in_specs=in_specs, out_specs=out_specs, check_vma=False)
```

```python
import functools

import jax
import jax.numpy as jnp
from jax import lax
from jax.experimental import pallas as pl
from jax.experimental.pallas import tpu as pltpu
from jax.sharding import PartitionSpec as P

TILE = 128
CHUNK = 128
BLOCK = 256
FLIGHT = 3
MESH = pl.DeviceIdType.MESH

learn_rate = 0.05
weight_decay = 0.02
user_scale = 1.0 / 64.0


def kernel(
    steps, cycle, groups,
    ids_ref, count_ref, users_hbm, panel_hbm, ratings_hbm, panel_out, grad_out,
    slot_rows, slot_ref, users, total, residual, grad_in, held, ratings,
    load_sem, rate_sem, slot_sem, send_sem, recv_sem, out_sem, grad_send, grad_recv,
):
    rows, rank = users.shape
    items = held[0].shape[0]
    slots = ratings[0].shape[0]
    row_tiles, col_tiles = rows // TILE, items // TILE
    chunks = items // CHUNK
    wide = CHUNK // TILE
    share = rows // groups

    u = lax.axis_index("user")
    g = lax.axis_index("item")
    right, left = lax.rem(u + 1, cycle), lax.rem(u + cycle - 1, cycle)

    barrier = pltpu.get_barrier_semaphore()
    for neighbour in (left, right):
        pl.semaphore_signal(barrier, inc=1, device_id={"user": neighbour}, device_id_type=MESH)
    for d in range(1, groups):
        pl.semaphore_signal(
            barrier, inc=1, device_id={"item": lax.rem(g + d, groups)}, device_id_type=MESH
        )

    def part(c):
        return pl.ds(pl.multiple_of(c * CHUNK, CHUNK), CHUNK)

    load_users = pltpu.make_async_copy(users_hbm, users, load_sem.at[chunks])
    load_panel = [
        pltpu.make_async_copy(panel_hbm.at[part(c)], held[0].at[part(c)], load_sem.at[c])
        for c in range(chunks)
    ]
    load_rates = [
        pltpu.make_async_copy(ratings_hbm.at[s], ratings[s], rate_sem.at[s]) for s in range(steps)
    ]
    load_panel[0].start()
    load_users.start()
    load_rates[0].start()
    for c in range(1, chunks):
        load_panel[c].start()
    for s in range(1, steps):
        load_rates[s].start()

    def send(s, c):
        return pltpu.make_async_remote_copy(
            src_ref=held[s].at[part(c)],
            dst_ref=held[s + 1].at[part(c)],
            send_sem=send_sem.at[s, c],
            recv_sem=recv_sem.at[s, c],
            device_id={"user": right},
            device_id_type=MESH,
        )

    def write(c):
        return pltpu.make_async_copy(held[-1].at[part(c)], panel_out.at[part(c)], out_sem.at[c])

    tile = lax.broadcasted_iota(jnp.int32, (1, slot_rows.shape[1]), 1)
    for s in range(steps):
        slot_of = jnp.full(tile.shape, slots, jnp.int32)
        for k in range(slots):
            listed = jnp.where(k < count_ref[s], ids_ref[s, 0, k], -1)
            slot_of = jnp.where(tile == listed, k, slot_of)
        slot_rows[s : s + 1, :] = slot_of
    map_slots = pltpu.make_async_copy(slot_rows, slot_ref, slot_sem)
    map_slots.start()

    def residuals(s, c, rounded):
        for top in range(0, rows, BLOCK):
            predicted = lax.dot_general(
                users[top : top + BLOCK, :], rounded, (((1,), (1,)), ((), ())),
                preferred_element_type=jnp.float32,
            )
            for i in range(BLOCK // TILE):
                for j in range(wide):
                    slot = slot_ref[s, (top // TILE + i) * col_tiles + c * wide + j]
                    live = (slot < slots).astype(jnp.float32)
                    rated = ratings[s][jnp.minimum(slot, slots - 1)].astype(jnp.float32)
                    guess = predicted[i * TILE : (i + 1) * TILE, j * TILE : (j + 1) * TILE]
                    residual[
                        top + i * TILE : top + (i + 1) * TILE, j * TILE : (j + 1) * TILE
                    ] = ((guess - rated) * live).astype(jnp.bfloat16)

    def update(s, c, panel):
        item_grad = lax.dot_general(
            residual[...], users[...], (((0,), (0,)), ((), ())),
            preferred_element_type=jnp.float32,
        )
        held[s][part(c), :] = panel - learn_rate * (item_grad + weight_decay * panel)

    def add_users(rounded, start, size):
        step = min(size, BLOCK)
        for offset in range(0, size, step):
            here = pl.ds(pl.multiple_of(start + offset, step), step)
            total[here, :] += jnp.dot(
                residual[here, :], rounded, preferred_element_type=jnp.float32
            )

    total[...] = jnp.zeros_like(total)
    map_slots.wait()
    load_users.wait()
    for s in range(steps):
        load_rates[s].wait()

        def work(c, carry, s=s):
            if s == 0:
                pltpu.make_async_copy(
                    panel_hbm.at[part(c)], held[0].at[part(c)], load_sem.at[c]
                ).wait()
            else:
                send(s - 1, c).wait_recv()
            panel = held[s][part(c), :]
            rounded = panel.astype(jnp.bfloat16)
            residuals(s, c, rounded)
            update(s, c, panel)
            if s < steps - 1:
                if s == 0:
                    @pl.when(c == 0)
                    def _():
                        pl.semaphore_wait(barrier, 2 + groups - 1)

                    @pl.when(c >= FLIGHT)
                    def _():
                        send(0, c - FLIGHT).wait_send()
                else:
                    @pl.when(c >= FLIGHT)
                    def _():
                        send(s, c - FLIGHT).wait_send()

                    @pl.when(c < FLIGHT)
                    def _():
                        send(s - 1, chunks + c - FLIGHT).wait_send()
                send(s, c).start()
            else:
                write(c).start()
            add_users(rounded, 0, rows)
            return carry

        lax.fori_loop(0, chunks if s < steps - 1 else chunks - 1, work, 0)

    def exchange(d):
        peer = lax.rem(g + d, groups)
        return pltpu.make_async_remote_copy(
            src_ref=total.at[pl.ds(pl.multiple_of(peer * share, share), share)],
            dst_ref=grad_in.at[d - 1],
            send_sem=grad_send.at[d - 1],
            recv_sem=grad_recv.at[d - 1],
            device_id={"item": peer},
            device_id_type=MESH,
        )

    final, last = steps - 1, chunks - 1
    send(final - 1, last).wait_recv()
    panel = held[final][part(last), :]
    rounded = panel.astype(jnp.bfloat16)
    residuals(final, last, rounded)
    for d in range(1, groups):
        add_users(rounded, lax.rem(g + d, groups) * share, share)
        exchange(d).start()
    update(final, last, panel)
    write(last).start()
    add_users(rounded, g * share, share)
    mine = pl.ds(pl.multiple_of(g * share, share), share)
    for d in range(1, groups):
        exchange(d).wait_recv()
        total[mine, :] += grad_in[d - 1]
    total[mine, :] = user_scale * total[mine, :]
    finish = pltpu.make_async_copy(total.at[mine], grad_out, load_sem.at[chunks])
    finish.start()
    for d in range(1, groups):
        exchange(d).wait_send()
    for c in range(chunks - FLIGHT, chunks):
        send(final - 1, c).wait_send()
    for c in range(chunks):
        write(c).wait()
    finish.wait()


def shards(user_factors, item_panels, ratings, tile_ids, tile_count):
    cycle, groups = lax.axis_size("user"), lax.axis_size("item")
    rows, rank = user_factors.shape
    items = item_panels.shape[0]
    steps, slots = ratings.shape[:2]
    chunks = items // CHUNK
    tiles = (rows // TILE) * (items // TILE)
    share = rows // groups

    ids = tile_ids.reshape(steps, 1, slots)
    count = tile_count.reshape(steps)

    scalars = pl.BlockSpec(memory_space=pltpu.SMEM)
    distant = pl.BlockSpec(memory_space=pltpu.HBM)
    anywhere = pl.BlockSpec(memory_space=pl.ANY)
    return pl.pallas_call(
        functools.partial(kernel, steps, cycle, groups),
        out_shape=(
            jax.ShapeDtypeStruct((items, rank), jnp.float32),
            jax.ShapeDtypeStruct((share, rank), jnp.float32),
        ),
        in_specs=[scalars] * 2 + [distant] * 3,
        out_specs=(anywhere, anywhere),
        scratch_shapes=[
            pltpu.VMEM((steps, tiles), jnp.int32),
            pltpu.SMEM((steps, tiles), jnp.int32),
            pltpu.VMEM((rows, rank), jnp.bfloat16),
            pltpu.VMEM((rows, rank), jnp.float32),
            pltpu.VMEM((rows, CHUNK), jnp.bfloat16),
            pltpu.VMEM((max(groups - 1, 1), share, rank), jnp.float32),
            [pltpu.VMEM((items, rank), jnp.float32) for _ in range(steps)],
            [pltpu.VMEM((slots, TILE, TILE), jnp.bfloat16) for _ in range(steps)],
            pltpu.SemaphoreType.DMA((chunks + 1,)),
            pltpu.SemaphoreType.DMA((steps,)),
            pltpu.SemaphoreType.DMA,
            pltpu.SemaphoreType.DMA((steps - 1, chunks)),
            pltpu.SemaphoreType.DMA((steps - 1, chunks)),
            pltpu.SemaphoreType.DMA((chunks,)),
            pltpu.SemaphoreType.DMA((max(groups - 1, 1),)),
            pltpu.SemaphoreType.DMA((max(groups - 1, 1),)),
        ],
        compiler_params=pltpu.CompilerParams(
            collective_id=0, has_side_effects=True, vmem_limit_bytes=62 * 2**20
        ),
        name="sub_epoch",
    )(ids, count, user_factors, item_panels, ratings)


def solution(mesh):
    in_specs = (
        P("user", None),
        P(("user", "item"), None),
        P(None, "user", "item", None),
        P(None, "user", "item"),
        P(None, "user", "item"),
    )
    out_specs = (P(("user", "item"), None), P(("user", "item"), None))
    return jax.shard_map(shards, mesh=mesh, in_specs=in_specs, out_specs=out_specs, check_vma=False)
```

```python
import functools

import jax
import jax.numpy as jnp
from jax import lax
from jax.experimental import pallas as pl
from jax.experimental.pallas import tpu as pltpu
from jax.sharding import PartitionSpec as P

TILE = 128
CHUNK = 128
BLOCK = 256
FLIGHT = 2
PIECES = 4
MESH = pl.DeviceIdType.MESH

learn_rate = 0.05
weight_decay = 0.02
user_scale = 1.0 / 64.0


def kernel(
    steps, cycle, groups,
    ids_ref, count_ref, users_hbm, panel_hbm, ratings_hbm, panel_out, grad_out,
    slot_rows, slot_ref, users, total, residual, grad_in, held, ratings,
    load_sem, rate_sem, slot_sem, send_sem, recv_sem, out_sem, grad_send, grad_recv,
):
    rows, rank = users.shape
    items = held[0].shape[0]
    slots = ratings[0].shape[0]
    row_tiles, col_tiles = rows // TILE, items // TILE
    chunks = items // CHUNK
    wide = CHUNK // TILE
    share = rows // groups

    u = lax.axis_index("user")
    g = lax.axis_index("item")
    right, left = lax.rem(u + 1, cycle), lax.rem(u + cycle - 1, cycle)

    barrier = pltpu.get_barrier_semaphore()
    pl.semaphore_signal(barrier, inc=1, device_id={"user": left}, device_id_type=MESH)
    for d in range(1, groups):
        pl.semaphore_signal(
            barrier, inc=1, device_id={"item": lax.rem(g + d, groups)}, device_id_type=MESH
        )

    def part(c):
        return pl.ds(pl.multiple_of(c * CHUNK, CHUNK), CHUNK)

    load_users = pltpu.make_async_copy(users_hbm, users, load_sem.at[chunks])
    load_panel = [
        pltpu.make_async_copy(panel_hbm.at[part(c)], held[0].at[part(c)], load_sem.at[c])
        for c in range(chunks)
    ]
    load_rates = [
        pltpu.make_async_copy(ratings_hbm.at[s], ratings[s], rate_sem.at[s]) for s in range(steps)
    ]
    load_panel[0].start()
    load_users.start()
    load_rates[0].start()
    for c in range(1, chunks):
        load_panel[c].start()
    for s in range(1, steps):
        load_rates[s].start()

    def send(s, c):
        return pltpu.make_async_remote_copy(
            src_ref=held[s].at[part(c)],
            dst_ref=held[s + 1].at[part(c)],
            send_sem=send_sem.at[s, c],
            recv_sem=recv_sem.at[s, c],
            device_id={"user": right},
            device_id_type=MESH,
        )

    def write(c):
        return pltpu.make_async_copy(held[-1].at[part(c)], panel_out.at[part(c)], out_sem.at[c])

    tile = lax.broadcasted_iota(jnp.int32, (1, slot_rows.shape[1]), 1)
    for s in range(steps):
        slot_of = jnp.full(tile.shape, slots, jnp.int32)
        for k in range(slots):
            listed = jnp.where(k < count_ref[s], ids_ref[s, 0, k], -1)
            slot_of = jnp.where(tile == listed, k, slot_of)
        slot_rows[s : s + 1, :] = slot_of
    map_slots = pltpu.make_async_copy(slot_rows, slot_ref, slot_sem)
    map_slots.start()

    def residuals(s, c, rounded):
        for top in range(0, rows, BLOCK):
            predicted = lax.dot_general(
                users[top : top + BLOCK, :], rounded, (((1,), (1,)), ((), ())),
                preferred_element_type=jnp.float32,
            )
            for i in range(BLOCK // TILE):
                for j in range(wide):
                    slot = slot_ref[s, (top // TILE + i) * col_tiles + c * wide + j]
                    live = (slot < slots).astype(jnp.float32)
                    rated = ratings[s][jnp.minimum(slot, slots - 1)].astype(jnp.float32)
                    guess = predicted[i * TILE : (i + 1) * TILE, j * TILE : (j + 1) * TILE]
                    residual[
                        top + i * TILE : top + (i + 1) * TILE, j * TILE : (j + 1) * TILE
                    ] = ((guess - rated) * live).astype(jnp.bfloat16)

    def update(s, c, panel):
        item_grad = lax.dot_general(
            residual[...], users[...], (((0,), (0,)), ((), ())),
            preferred_element_type=jnp.float32,
        )
        held[s][part(c), :] = panel - learn_rate * (item_grad + weight_decay * panel)

    def add_users(rounded, start, size):
        step = min(size, BLOCK)
        for offset in range(0, size, step):
            here = pl.ds(pl.multiple_of(start + offset, step), step)
            total[here, :] += jnp.dot(
                residual[here, :], rounded, preferred_element_type=jnp.float32
            )

    total[...] = jnp.zeros_like(total)
    map_slots.wait()
    load_users.wait()
    for s in range(steps):
        load_rates[s].wait()

        def work(c, carry, s=s):
            if s == 0:
                pltpu.make_async_copy(
                    panel_hbm.at[part(c)], held[0].at[part(c)], load_sem.at[c]
                ).wait()
            else:
                send(s - 1, c).wait_recv()
            panel = held[s][part(c), :]
            rounded = panel.astype(jnp.bfloat16)
            residuals(s, c, rounded)
            update(s, c, panel)
            if s < steps - 1:
                if s == 0:
                    @pl.when(c == 0)
                    def _():
                        pl.semaphore_wait(barrier, groups)

                    @pl.when(c >= FLIGHT)
                    def _():
                        send(0, c - FLIGHT).wait_send()
                else:
                    @pl.when(c >= FLIGHT)
                    def _():
                        send(s, c - FLIGHT).wait_send()

                    @pl.when(c < FLIGHT)
                    def _():
                        send(s - 1, chunks + c - FLIGHT).wait_send()
                send(s, c).start()
            else:
                write(c).start()
            add_users(rounded, 0, rows)
            return carry

        lax.fori_loop(0, chunks if s < steps - 1 else chunks - 1, work, 0)

    def exchange(d):
        peer = lax.rem(g + d, groups)
        return pltpu.make_async_remote_copy(
            src_ref=total.at[pl.ds(pl.multiple_of(peer * share, share), share)],
            dst_ref=grad_in.at[d - 1],
            send_sem=grad_send.at[d - 1],
            recv_sem=grad_recv.at[d - 1],
            device_id={"item": peer},
            device_id_type=MESH,
        )

    final, last = steps - 1, chunks - 1
    send(final - 1, last).wait_recv()
    panel = held[final][part(last), :]
    rounded = panel.astype(jnp.bfloat16)
    residuals(final, last, rounded)
    for d in range(1, groups):
        add_users(rounded, lax.rem(g + d, groups) * share, share)
        exchange(d).start()
    update(final, last, panel)
    write(last).start()
    add_users(rounded, g * share, share)
    mine = pl.ds(pl.multiple_of(g * share, share), share)
    for d in range(1, groups):
        exchange(d).wait_recv()
        total[mine, :] += grad_in[d - 1]
    total[mine, :] = user_scale * total[mine, :]
    finish = pltpu.make_async_copy(total.at[mine], grad_out, load_sem.at[chunks])
    finish.start()
    for d in range(1, groups):
        exchange(d).wait_send()
    for c in range(chunks - FLIGHT, chunks):
        send(final - 1, c).wait_send()
    for c in range(chunks):
        write(c).wait()
    finish.wait()


def place(held, gradient, panel_out, grad_out, panel_sem, grad_sem):
    copies = []
    for source, target, sem in ((held, panel_out, panel_sem), (gradient, grad_out, grad_sem)):
        size = source.shape[0] // PIECES
        for piece in range(PIECES):
            here = pl.ds(piece * size, size)
            copies.append(
                pltpu.make_async_copy(source.at[here], target.at[here], sem.at[piece])
            )
    for copy in copies:
        copy.start()
    for copy in copies:
        copy.wait()


def shards(user_factors, item_panels, ratings, tile_ids, tile_count):
    cycle, groups = lax.axis_size("user"), lax.axis_size("item")
    rows, rank = user_factors.shape
    items = item_panels.shape[0]
    steps, slots = ratings.shape[:2]
    chunks = items // CHUNK
    tiles = (rows // TILE) * (items // TILE)
    share = rows // groups

    ids = tile_ids.reshape(steps, 1, slots)
    count = tile_count.reshape(steps)

    scalars = pl.BlockSpec(memory_space=pltpu.SMEM)
    distant = pl.BlockSpec(memory_space=pltpu.HBM)
    anywhere = pl.BlockSpec(memory_space=pl.ANY)
    held, gradient = pl.pallas_call(
        functools.partial(kernel, steps, cycle, groups),
        out_shape=(
            pltpu.VMEM((items, rank), jnp.float32),
            pltpu.VMEM((share, rank), jnp.float32),
        ),
        in_specs=[scalars] * 2 + [distant] * 3,
        out_specs=(anywhere, anywhere),
        scratch_shapes=[
            pltpu.VMEM((steps, tiles), jnp.int32),
            pltpu.SMEM((steps, tiles), jnp.int32),
            pltpu.VMEM((rows, rank), jnp.bfloat16),
            pltpu.VMEM((rows, rank), jnp.float32),
            pltpu.VMEM((rows, CHUNK), jnp.bfloat16),
            pltpu.VMEM((max(groups - 1, 1), share, rank), jnp.float32),
            [pltpu.VMEM((items, rank), jnp.float32) for _ in range(steps)],
            [pltpu.VMEM((slots, TILE, TILE), jnp.bfloat16) for _ in range(steps)],
            pltpu.SemaphoreType.DMA((chunks + 1,)),
            pltpu.SemaphoreType.DMA((steps,)),
            pltpu.SemaphoreType.DMA,
            pltpu.SemaphoreType.DMA((steps - 1, chunks)),
            pltpu.SemaphoreType.DMA((steps - 1, chunks)),
            pltpu.SemaphoreType.DMA((chunks,)),
            pltpu.SemaphoreType.DMA((max(groups - 1, 1),)),
            pltpu.SemaphoreType.DMA((max(groups - 1, 1),)),
        ],
        compiler_params=pltpu.CompilerParams(
            collective_id=0, has_side_effects=True, vmem_limit_bytes=56 * 2**20
        ),
        name="sub_epoch",
    )(
        ids, count,
        *(pltpu.with_memory_space_constraint(x, pltpu.HBM) for x in (user_factors, item_panels, ratings)),
    )
    return pl.pallas_call(
        place,
        out_shape=(
            jax.ShapeDtypeStruct(held.shape, held.dtype),
            jax.ShapeDtypeStruct(gradient.shape, gradient.dtype),
        ),
        in_specs=[anywhere] * 2,
        out_specs=(anywhere, anywhere),
        scratch_shapes=[pltpu.SemaphoreType.DMA((PIECES,)), pltpu.SemaphoreType.DMA((PIECES,))],
        name="place",
    )(held, gradient)


def solution(mesh):
    in_specs = (
        P("user", None),
        P(("user", "item"), None),
        P(None, "user", "item", None),
        P(None, "user", "item"),
        P(None, "user", "item"),
    )
    out_specs = (P(("user", "item"), None), P(("user", "item"), None))
    return jax.shard_map(shards, mesh=mesh, in_specs=in_specs, out_specs=out_specs, check_vma=False)
```

```python
import functools

import jax
import jax.numpy as jnp
from jax import lax
from jax.experimental import pallas as pl
from jax.experimental.pallas import tpu as pltpu
from jax.sharding import PartitionSpec as P

TILE = 128
CHUNK = 128
BLOCK = 256
FLIGHT = 4
PIECES = 4
MESH = pl.DeviceIdType.MESH

learn_rate = 0.05
weight_decay = 0.02
user_scale = 1.0 / 64.0


def kernel(
    steps, cycle, groups,
    ids_ref, count_ref, users_hbm, panel_hbm, ratings_hbm, panel_out, grad_out,
    slot_rows, slot_ref, users, total, residual, grad_in, held, ratings,
    load_sem, rate_sem, slot_sem, send_sem, recv_sem, out_sem, grad_sem, grad_send, grad_recv,
):
    rows, rank = users.shape
    items = held[0].shape[0]
    slots = ratings[0].shape[0]
    row_tiles, col_tiles = rows // TILE, items // TILE
    chunks = items // CHUNK
    wide = CHUNK // TILE
    share = rows // groups

    u = lax.axis_index("user")
    g = lax.axis_index("item")
    right, left = lax.rem(u + 1, cycle), lax.rem(u + cycle - 1, cycle)

    barrier = pltpu.get_barrier_semaphore()
    pl.semaphore_signal(barrier, inc=1, device_id={"user": left}, device_id_type=MESH)
    for d in range(1, groups):
        pl.semaphore_signal(
            barrier, inc=1, device_id={"item": lax.rem(g + d, groups)}, device_id_type=MESH
        )

    def part(c):
        return pl.ds(pl.multiple_of(c * CHUNK, CHUNK), CHUNK)

    load_users = pltpu.make_async_copy(users_hbm, users, load_sem.at[chunks])
    load_panel = [
        pltpu.make_async_copy(panel_hbm.at[part(c)], held[0].at[part(c)], load_sem.at[c])
        for c in range(chunks)
    ]
    load_rates = [
        pltpu.make_async_copy(ratings_hbm.at[s], ratings[s], rate_sem.at[s]) for s in range(steps)
    ]
    load_panel[0].start()
    load_users.start()
    load_rates[0].start()
    for c in range(1, chunks):
        load_panel[c].start()
    for s in range(1, steps):
        load_rates[s].start()

    def send(s, c):
        return pltpu.make_async_remote_copy(
            src_ref=held[s].at[part(c)],
            dst_ref=held[s + 1].at[part(c)],
            send_sem=send_sem.at[s, c],
            recv_sem=recv_sem.at[s, c],
            device_id={"user": right},
            device_id_type=MESH,
        )

    def write(c):
        return pltpu.make_async_copy(held[-1].at[part(c)], panel_out.at[part(c)], out_sem.at[c])

    tile = lax.broadcasted_iota(jnp.int32, (1, slot_rows.shape[1]), 1)
    for s in range(steps):
        slot_of = jnp.full(tile.shape, slots, jnp.int32)
        for k in range(slots):
            listed = jnp.where(k < count_ref[s], ids_ref[s, 0, k], -1)
            slot_of = jnp.where(tile == listed, k, slot_of)
        slot_rows[s : s + 1, :] = slot_of
    map_slots = pltpu.make_async_copy(slot_rows, slot_ref, slot_sem)
    map_slots.start()

    def residuals(s, c, rounded, start, size):
        step = min(size, BLOCK)
        for offset in range(0, size, step):
            top = pl.multiple_of(start + offset, step)
            predicted = lax.dot_general(
                users[pl.ds(top, step), :], rounded, (((1,), (1,)), ((), ())),
                preferred_element_type=jnp.float32,
            )
            for i in range(step // TILE):
                for j in range(wide):
                    slot = slot_ref[s, (top // TILE + i) * col_tiles + c * wide + j]
                    live = (slot < slots).astype(jnp.float32)
                    rated = ratings[s][jnp.minimum(slot, slots - 1)].astype(jnp.float32)
                    guess = predicted[i * TILE : (i + 1) * TILE, j * TILE : (j + 1) * TILE]
                    residual[
                        pl.ds(pl.multiple_of(top + i * TILE, TILE), TILE),
                        j * TILE : (j + 1) * TILE,
                    ] = ((guess - rated) * live).astype(jnp.bfloat16)

    def update(s, c, panel):
        item_grad = lax.dot_general(
            residual[...], users[...], (((0,), (0,)), ((), ())),
            preferred_element_type=jnp.float32,
        )
        held[s][part(c), :] = panel - learn_rate * (item_grad + weight_decay * panel)

    def add_users(rounded, start, size):
        step = min(size, BLOCK)
        for offset in range(0, size, step):
            here = pl.ds(pl.multiple_of(start + offset, step), step)
            total[here, :] += jnp.dot(
                residual[here, :], rounded, preferred_element_type=jnp.float32
            )

    total[...] = jnp.zeros_like(total)
    map_slots.wait()
    load_users.wait()
    for s in range(steps):
        load_rates[s].wait()

        def work(c, carry, s=s):
            if s == 0:
                pltpu.make_async_copy(
                    panel_hbm.at[part(c)], held[0].at[part(c)], load_sem.at[c]
                ).wait()
            else:
                send(s - 1, c).wait_recv()
            panel = held[s][part(c), :]
            rounded = panel.astype(jnp.bfloat16)
            residuals(s, c, rounded, 0, rows)
            update(s, c, panel)
            if s < steps - 1:
                if s == 0:
                    @pl.when(c == 0)
                    def _():
                        pl.semaphore_wait(barrier, groups)

                    @pl.when(c >= FLIGHT)
                    def _():
                        send(0, c - FLIGHT).wait_send()
                else:
                    @pl.when(c >= FLIGHT)
                    def _():
                        send(s, c - FLIGHT).wait_send()

                    @pl.when(c < FLIGHT)
                    def _():
                        send(s - 1, chunks + c - FLIGHT).wait_send()
                send(s, c).start()
            else:
                write(c).start()
            add_users(rounded, 0, rows)
            return carry

        lax.fori_loop(0, chunks if s < steps - 1 else chunks - 1, work, 0)

    block = min(share, BLOCK)

    def exchange(d, b):
        peer = lax.rem(g + d, groups)
        top = pl.multiple_of(peer * share + b * block, block)
        return pltpu.make_async_remote_copy(
            src_ref=total.at[pl.ds(top, block)],
            dst_ref=grad_in.at[d - 1, pl.ds(b * block, block)],
            send_sem=grad_send.at[d - 1, b],
            recv_sem=grad_recv.at[d - 1, b],
            device_id={"item": peer},
            device_id_type=MESH,
        )

    def finish(b):
        here = pl.ds(pl.multiple_of(g * share + b * block, block), block)
        return here, pltpu.make_async_copy(
            total.at[here], grad_out.at[pl.ds(b * block, block)], grad_sem.at[b]
        )

    final, last = steps - 1, chunks - 1
    send(final - 1, last).wait_recv()
    panel = held[final][part(last), :]
    rounded = panel.astype(jnp.bfloat16)
    parts = [(d, b) for d in range(1, groups) for b in range(share // block)]
    for d, b in parts:
        top = lax.rem(g + d, groups) * share + b * block
        residuals(final, last, rounded, top, block)
        add_users(rounded, top, block)
        exchange(d, b).start()
    residuals(final, last, rounded, g * share, share)
    update(final, last, panel)
    write(last).start()
    add_users(rounded, g * share, share)
    for b in range(share // block):
        here, done = finish(b)
        for d in range(1, groups):
            exchange(d, b).wait_recv()
            total[here, :] += grad_in[d - 1, pl.ds(b * block, block), :]
        total[here, :] = user_scale * total[here, :]
        done.start()
    for d, b in parts:
        exchange(d, b).wait_send()
    for c in range(chunks - FLIGHT, chunks):
        send(final - 1, c).wait_send()
    for c in range(chunks):
        write(c).wait()
    for b in range(share // block):
        finish(b)[1].wait()


def place(held, gradient, panel_out, grad_out, panel_sem, grad_sem):
    copies = []
    for source, target, sem in ((held, panel_out, panel_sem), (gradient, grad_out, grad_sem)):
        size = source.shape[0] // PIECES
        for piece in range(PIECES):
            here = pl.ds(piece * size, size)
            copies.append(
                pltpu.make_async_copy(source.at[here], target.at[here], sem.at[piece])
            )
    for copy in copies:
        copy.start()
    for copy in copies:
        copy.wait()


def shards(user_factors, item_panels, ratings, tile_ids, tile_count):
    cycle, groups = lax.axis_size("user"), lax.axis_size("item")
    rows, rank = user_factors.shape
    items = item_panels.shape[0]
    steps, slots = ratings.shape[:2]
    chunks = items // CHUNK
    tiles = (rows // TILE) * (items // TILE)
    share = rows // groups
    blocks = share // min(share, BLOCK)

    ids = tile_ids.reshape(steps, 1, slots)
    count = tile_count.reshape(steps)

    scalars = pl.BlockSpec(memory_space=pltpu.SMEM)
    distant = pl.BlockSpec(memory_space=pltpu.HBM)
    anywhere = pl.BlockSpec(memory_space=pl.ANY)
    held, gradient = pl.pallas_call(
        functools.partial(kernel, steps, cycle, groups),
        out_shape=(
            pltpu.VMEM((items, rank), jnp.float32),
            pltpu.VMEM((share, rank), jnp.float32),
        ),
        in_specs=[scalars] * 2 + [distant] * 3,
        out_specs=(anywhere, anywhere),
        scratch_shapes=[
            pltpu.VMEM((steps, tiles), jnp.int32),
            pltpu.SMEM((steps, tiles), jnp.int32),
            pltpu.VMEM((rows, rank), jnp.bfloat16),
            pltpu.VMEM((rows, rank), jnp.float32),
            pltpu.VMEM((rows, CHUNK), jnp.bfloat16),
            pltpu.VMEM((max(groups - 1, 1), share, rank), jnp.float32),
            [pltpu.VMEM((items, rank), jnp.float32) for _ in range(steps)],
            [pltpu.VMEM((slots, TILE, TILE), jnp.bfloat16) for _ in range(steps)],
            pltpu.SemaphoreType.DMA((chunks + 1,)),
            pltpu.SemaphoreType.DMA((steps,)),
            pltpu.SemaphoreType.DMA,
            pltpu.SemaphoreType.DMA((steps - 1, chunks)),
            pltpu.SemaphoreType.DMA((steps - 1, chunks)),
            pltpu.SemaphoreType.DMA((chunks,)),
            pltpu.SemaphoreType.DMA((blocks,)),
            pltpu.SemaphoreType.DMA((max(groups - 1, 1), blocks)),
            pltpu.SemaphoreType.DMA((max(groups - 1, 1), blocks)),
        ],
        compiler_params=pltpu.CompilerParams(
            collective_id=0, has_side_effects=True, vmem_limit_bytes=56 * 2**20
        ),
        name="sub_epoch",
    )(
        ids, count,
        *(pltpu.with_memory_space_constraint(x, pltpu.HBM) for x in (user_factors, item_panels, ratings)),
    )
    return pl.pallas_call(
        place,
        out_shape=(
            jax.ShapeDtypeStruct(held.shape, held.dtype),
            jax.ShapeDtypeStruct(gradient.shape, gradient.dtype),
        ),
        in_specs=[anywhere] * 2,
        out_specs=(anywhere, anywhere),
        scratch_shapes=[pltpu.SemaphoreType.DMA((PIECES,)), pltpu.SemaphoreType.DMA((PIECES,))],
        compiler_params=pltpu.CompilerParams(vmem_limit_bytes=4 * 2**20),
        name="place",
    )(*(pltpu.with_memory_space_constraint(x, pltpu.VMEM) for x in (held, gradient)))


def solution(mesh):
    in_specs = (
        P("user", None),
        P(("user", "item"), None),
        P(None, "user", "item", None),
        P(None, "user", "item"),
        P(None, "user", "item"),
    )
    out_specs = (P(("user", "item"), None), P(("user", "item"), None))
    return jax.shard_map(shards, mesh=mesh, in_specs=in_specs, out_specs=out_specs, check_vma=False)
```

```python
import functools

import jax
import jax.numpy as jnp
from jax import lax
from jax.experimental import pallas as pl
from jax.experimental.pallas import tpu as pltpu
from jax.sharding import PartitionSpec as P

TILE = 128
CHUNK = 128
BLOCK = 256
FLIGHT = 4
PIECES = 4
MESH = pl.DeviceIdType.MESH

learn_rate = 0.05
weight_decay = 0.02
user_scale = 1.0 / 64.0


def kernel(
    steps, cycle, groups,
    ids_ref, count_ref, users_hbm, panel_hbm, ratings_hbm, panel_out, grad_out,
    slot_rows, slot_ref, detour, users, total, residual, grad_in, held, ratings,
    load_sem, rate_sem, slot_sem, send_sem, recv_sem, out_sem, grad_sem, grad_send, grad_recv,
    detour_send, detour_recv,
):
    rows, rank = users.shape
    items = held[0].shape[0]
    slots = ratings[0].shape[0]
    row_tiles, col_tiles = rows // TILE, items // TILE
    chunks = items // CHUNK
    wide = CHUNK // TILE
    share = rows // groups

    u = lax.axis_index("user")
    g = lax.axis_index("item")
    right, left = lax.rem(u + 1, cycle), lax.rem(u + cycle - 1, cycle)

    barrier = pltpu.get_barrier_semaphore()
    pl.semaphore_signal(barrier, inc=1, device_id={"user": left}, device_id_type=MESH)
    for d in range(1, groups):
        pl.semaphore_signal(
            barrier, inc=1, device_id={"item": lax.rem(g + d, groups)}, device_id_type=MESH
        )

    first, helper, end = 0, 1, cycle - 1
    helped = cycle > 3
    if helped:
        for source, target in ((first, helper), (helper, end)):
            @pl.when(u == source)
            def _(target=target):
                pl.semaphore_signal(barrier, inc=1, device_id={"user": target}, device_id_type=MESH)

    def part(c):
        return pl.ds(pl.multiple_of(c * CHUNK, CHUNK), CHUNK)

    load_users = pltpu.make_async_copy(users_hbm, users, load_sem.at[chunks])
    load_panel = [
        pltpu.make_async_copy(panel_hbm.at[part(c)], held[0].at[part(c)], load_sem.at[c])
        for c in range(chunks)
    ]
    load_rates = [
        pltpu.make_async_copy(ratings_hbm.at[s], ratings[s], rate_sem.at[s]) for s in range(steps)
    ]
    load_panel[0].start()
    load_users.start()
    load_rates[0].start()
    for c in range(1, chunks):
        load_panel[c].start()
    for s in range(1, steps):
        load_rates[s].start()

    def send(s, c):
        return pltpu.make_async_remote_copy(
            src_ref=held[s].at[part(c)],
            dst_ref=held[s + 1].at[part(c)],
            send_sem=send_sem.at[s, c],
            recv_sem=recv_sem.at[s, c],
            device_id={"user": right},
            device_id_type=MESH,
        )

    def aside():
        return pltpu.make_async_remote_copy(
            src_ref=held[0].at[part(chunks - 1)],
            dst_ref=detour,
            send_sem=send_sem.at[0, chunks - 1],
            recv_sem=detour_recv,
            device_id={"user": helper},
            device_id_type=MESH,
        )

    def onward():
        return pltpu.make_async_remote_copy(
            src_ref=detour,
            dst_ref=held[1].at[part(chunks - 1)],
            send_sem=detour_send,
            recv_sem=recv_sem.at[0, chunks - 1],
            device_id={"user": first},
            device_id_type=MESH,
        )

    def write(c):
        return pltpu.make_async_copy(held[-1].at[part(c)], panel_out.at[part(c)], out_sem.at[c])

    tile = lax.broadcasted_iota(jnp.int32, (1, slot_rows.shape[1]), 1)
    for s in range(steps):
        slot_of = jnp.full(tile.shape, slots, jnp.int32)
        for k in range(slots):
            listed = jnp.where(k < count_ref[s], ids_ref[s, 0, k], -1)
            slot_of = jnp.where(tile == listed, k, slot_of)
        slot_rows[s : s + 1, :] = slot_of
    map_slots = pltpu.make_async_copy(slot_rows, slot_ref, slot_sem)
    map_slots.start()

    def residuals(s, c, rounded, start, size):
        step = min(size, BLOCK)
        for offset in range(0, size, step):
            top = pl.multiple_of(start + offset, step)
            predicted = lax.dot_general(
                users[pl.ds(top, step), :], rounded, (((1,), (1,)), ((), ())),
                preferred_element_type=jnp.float32,
            )
            for i in range(step // TILE):
                for j in range(wide):
                    slot = slot_ref[s, (top // TILE + i) * col_tiles + c * wide + j]
                    live = (slot < slots).astype(jnp.float32)
                    rated = ratings[s][jnp.minimum(slot, slots - 1)].astype(jnp.float32)
                    guess = predicted[i * TILE : (i + 1) * TILE, j * TILE : (j + 1) * TILE]
                    residual[
                        pl.ds(pl.multiple_of(top + i * TILE, TILE), TILE),
                        j * TILE : (j + 1) * TILE,
                    ] = ((guess - rated) * live).astype(jnp.bfloat16)

    def update(s, c, panel):
        item_grad = lax.dot_general(
            residual[...], users[...], (((0,), (0,)), ((), ())),
            preferred_element_type=jnp.float32,
        )
        held[s][part(c), :] = panel - learn_rate * (item_grad + weight_decay * panel)

    def add_users(rounded, start, size):
        step = min(size, BLOCK)
        for offset in range(0, size, step):
            here = pl.ds(pl.multiple_of(start + offset, step), step)
            total[here, :] += jnp.dot(
                residual[here, :], rounded, preferred_element_type=jnp.float32
            )

    total[...] = jnp.zeros_like(total)
    map_slots.wait()
    load_users.wait()
    for s in range(steps):
        load_rates[s].wait()

        def work(c, carry, s=s):
            if s == 0:
                pltpu.make_async_copy(
                    panel_hbm.at[part(c)], held[0].at[part(c)], load_sem.at[c]
                ).wait()
            else:
                if s == 1 and helped:
                    @pl.when((u == helper) & (c == chunks // 2 + 1))
                    def _():
                        aside().wait_recv()
                        onward().start()
                send(s - 1, c).wait_recv()
            panel = held[s][part(c), :]
            rounded = panel.astype(jnp.bfloat16)
            residuals(s, c, rounded, 0, rows)
            update(s, c, panel)
            if s < steps - 1:
                if s == 0:
                    @pl.when(c == 0)
                    def _():
                        if helped:
                            aiding = (u == helper) | (u == end)

                            @pl.when(aiding)
                            def _():
                                pl.semaphore_wait(barrier, groups + 1)

                            @pl.when(jnp.logical_not(aiding))
                            def _():
                                pl.semaphore_wait(barrier, groups)
                        else:
                            pl.semaphore_wait(barrier, groups)

                    @pl.when(c >= FLIGHT)
                    def _():
                        send(0, c - FLIGHT).wait_send()
                else:
                    @pl.when(c >= FLIGHT)
                    def _():
                        send(s, c - FLIGHT).wait_send()

                    @pl.when(c < FLIGHT)
                    def _():
                        send(s - 1, chunks + c - FLIGHT).wait_send()
                if s == 0 and helped:
                    parted = (u == end) & (c == chunks - 1)

                    @pl.when(parted)
                    def _():
                        aside().start()

                    @pl.when(jnp.logical_not(parted))
                    def _():
                        send(s, c).start()
                else:
                    send(s, c).start()
            else:
                write(c).start()
            add_users(rounded, 0, rows)
            return carry

        lax.fori_loop(0, chunks if s < steps - 1 else chunks - 1, work, 0)

    block = min(share, BLOCK)

    def exchange(d, b):
        peer = lax.rem(g + d, groups)
        top = pl.multiple_of(peer * share + b * block, block)
        return pltpu.make_async_remote_copy(
            src_ref=total.at[pl.ds(top, block)],
            dst_ref=grad_in.at[d - 1, pl.ds(b * block, block)],
            send_sem=grad_send.at[d - 1, b],
            recv_sem=grad_recv.at[d - 1, b],
            device_id={"item": peer},
            device_id_type=MESH,
        )

    def finish(b):
        here = pl.ds(pl.multiple_of(g * share + b * block, block), block)
        return here, pltpu.make_async_copy(
            total.at[here], grad_out.at[pl.ds(b * block, block)], grad_sem.at[b]
        )

    final, last = steps - 1, chunks - 1
    send(final - 1, last).wait_recv()
    panel = held[final][part(last), :]
    rounded = panel.astype(jnp.bfloat16)
    parts = [(d, b) for d in range(1, groups) for b in range(share // block)]
    for d, b in parts:
        top = lax.rem(g + d, groups) * share + b * block
        residuals(final, last, rounded, top, block)
        add_users(rounded, top, block)
        exchange(d, b).start()
    residuals(final, last, rounded, g * share, share)
    update(final, last, panel)
    write(last).start()
    add_users(rounded, g * share, share)
    for b in range(share // block):
        here, done = finish(b)
        for d in range(1, groups):
            exchange(d, b).wait_recv()
            total[here, :] += grad_in[d - 1, pl.ds(b * block, block), :]
        total[here, :] = user_scale * total[here, :]
        done.start()
    for d, b in parts:
        exchange(d, b).wait_send()
    for c in range(chunks - FLIGHT, chunks):
        send(final - 1, c).wait_send()
    if helped:
        @pl.when(u == helper)
        def _():
            onward().wait_send()
    for c in range(chunks):
        write(c).wait()
    for b in range(share // block):
        finish(b)[1].wait()


def place(held, gradient, panel_out, grad_out, panel_sem, grad_sem):
    copies = []
    for source, target, sem in ((held, panel_out, panel_sem), (gradient, grad_out, grad_sem)):
        size = source.shape[0] // PIECES
        for piece in range(PIECES):
            here = pl.ds(piece * size, size)
            copies.append(
                pltpu.make_async_copy(source.at[here], target.at[here], sem.at[piece])
            )
    for copy in copies:
        copy.start()
    for copy in copies:
        copy.wait()


def shards(user_factors, item_panels, ratings, tile_ids, tile_count):
    cycle, groups = lax.axis_size("user"), lax.axis_size("item")
    rows, rank = user_factors.shape
    items = item_panels.shape[0]
    steps, slots = ratings.shape[:2]
    chunks = items // CHUNK
    tiles = (rows // TILE) * (items // TILE)
    share = rows // groups
    blocks = share // min(share, BLOCK)

    ids = tile_ids.reshape(steps, 1, slots)
    count = tile_count.reshape(steps)

    scalars = pl.BlockSpec(memory_space=pltpu.SMEM)
    distant = pl.BlockSpec(memory_space=pltpu.HBM)
    anywhere = pl.BlockSpec(memory_space=pl.ANY)
    held, gradient = pl.pallas_call(
        functools.partial(kernel, steps, cycle, groups),
        out_shape=(
            pltpu.VMEM((items, rank), jnp.float32),
            pltpu.VMEM((share, rank), jnp.float32),
        ),
        in_specs=[scalars] * 2 + [distant] * 3,
        out_specs=(anywhere, anywhere),
        scratch_shapes=[
            pltpu.VMEM((steps, tiles), jnp.int32),
            pltpu.SMEM((steps, tiles), jnp.int32),
            pltpu.VMEM((CHUNK, rank), jnp.float32),
            pltpu.VMEM((rows, rank), jnp.bfloat16),
            pltpu.VMEM((rows, rank), jnp.float32),
            pltpu.VMEM((rows, CHUNK), jnp.bfloat16),
            pltpu.VMEM((max(groups - 1, 1), share, rank), jnp.float32),
            [pltpu.VMEM((items, rank), jnp.float32) for _ in range(steps)],
            [pltpu.VMEM((slots, TILE, TILE), jnp.bfloat16) for _ in range(steps)],
            pltpu.SemaphoreType.DMA((chunks + 1,)),
            pltpu.SemaphoreType.DMA((steps,)),
            pltpu.SemaphoreType.DMA,
            pltpu.SemaphoreType.DMA((steps - 1, chunks)),
            pltpu.SemaphoreType.DMA((steps - 1, chunks)),
            pltpu.SemaphoreType.DMA((chunks,)),
            pltpu.SemaphoreType.DMA((blocks,)),
            pltpu.SemaphoreType.DMA((max(groups - 1, 1), blocks)),
            pltpu.SemaphoreType.DMA((max(groups - 1, 1), blocks)),
            pltpu.SemaphoreType.DMA,
            pltpu.SemaphoreType.DMA,
        ],
        compiler_params=pltpu.CompilerParams(
            collective_id=0, has_side_effects=True, vmem_limit_bytes=56 * 2**20
        ),
        name="sub_epoch",
    )(
        ids, count,
        *(pltpu.with_memory_space_constraint(x, pltpu.HBM) for x in (user_factors, item_panels, ratings)),
    )
    return pl.pallas_call(
        place,
        out_shape=(
            jax.ShapeDtypeStruct(held.shape, held.dtype),
            jax.ShapeDtypeStruct(gradient.shape, gradient.dtype),
        ),
        in_specs=[anywhere] * 2,
        out_specs=(anywhere, anywhere),
        scratch_shapes=[pltpu.SemaphoreType.DMA((PIECES,)), pltpu.SemaphoreType.DMA((PIECES,))],
        compiler_params=pltpu.CompilerParams(vmem_limit_bytes=4 * 2**20),
        name="place",
    )(*(pltpu.with_memory_space_constraint(x, pltpu.VMEM) for x in (held, gradient)))


def solution(mesh):
    in_specs = (
        P("user", None),
        P(("user", "item"), None),
        P(None, "user", "item", None),
        P(None, "user", "item"),
        P(None, "user", "item"),
    )
    out_specs = (P(("user", "item"), None), P(("user", "item"), None))
    return jax.shard_map(shards, mesh=mesh, in_specs=in_specs, out_specs=out_specs, check_vma=False)
```

```python
import functools

import jax
import jax.numpy as jnp
from jax import lax
from jax.experimental import pallas as pl
from jax.experimental.pallas import tpu as pltpu
from jax.sharding import PartitionSpec as P

TILE = 128
CHUNK = 256
BLOCK = 256
FLIGHT = 4
PIECES = 4
MESH = pl.DeviceIdType.MESH

learn_rate = 0.05
weight_decay = 0.02
user_scale = 1.0 / 64.0


def kernel(
    steps, cycle, groups,
    ids_ref, count_ref, users_hbm, panel_hbm, ratings_hbm, panel_out, grad_out,
    slot_rows, slot_ref, users, total, residual, grad_in, held, ratings,
    load_sem, rate_sem, slot_sem, send_sem, recv_sem, out_sem, grad_sem, grad_send, grad_recv,
):
    rows, rank = users.shape
    items = held[0].shape[0]
    slots = ratings[0].shape[0]
    row_tiles, col_tiles = rows // TILE, items // TILE
    chunks = items // CHUNK
    wide = CHUNK // TILE
    share = rows // groups

    u = lax.axis_index("user")
    g = lax.axis_index("item")
    right, left = lax.rem(u + 1, cycle), lax.rem(u + cycle - 1, cycle)

    barrier = pltpu.get_barrier_semaphore()
    pl.semaphore_signal(barrier, inc=1, device_id={"user": left}, device_id_type=MESH)
    for d in range(1, groups):
        pl.semaphore_signal(
            barrier, inc=1, device_id={"item": lax.rem(g + d, groups)}, device_id_type=MESH
        )

    def part(c):
        return pl.ds(pl.multiple_of(c * CHUNK, CHUNK), CHUNK)

    load_users = pltpu.make_async_copy(users_hbm, users, load_sem.at[chunks])
    load_panel = [
        pltpu.make_async_copy(panel_hbm.at[part(c)], held[0].at[part(c)], load_sem.at[c])
        for c in range(chunks)
    ]
    load_rates = [
        pltpu.make_async_copy(ratings_hbm.at[s], ratings[s], rate_sem.at[s]) for s in range(steps)
    ]
    load_panel[0].start()
    load_users.start()
    load_rates[0].start()
    for c in range(1, chunks):
        load_panel[c].start()
    for s in range(1, steps):
        load_rates[s].start()

    def send(s, c):
        return pltpu.make_async_remote_copy(
            src_ref=held[s].at[part(c)],
            dst_ref=held[s + 1].at[part(c)],
            send_sem=send_sem.at[s, c],
            recv_sem=recv_sem.at[s, c],
            device_id={"user": right},
            device_id_type=MESH,
        )

    def write(c):
        return pltpu.make_async_copy(held[-1].at[part(c)], panel_out.at[part(c)], out_sem.at[c])

    tile = lax.broadcasted_iota(jnp.int32, (1, slot_rows.shape[1]), 1)
    for s in range(steps):
        slot_of = jnp.full(tile.shape, slots, jnp.int32)
        for k in range(slots):
            listed = jnp.where(k < count_ref[s], ids_ref[s, 0, k], -1)
            slot_of = jnp.where(tile == listed, k, slot_of)
        slot_rows[s : s + 1, :] = slot_of
    map_slots = pltpu.make_async_copy(slot_rows, slot_ref, slot_sem)
    map_slots.start()

    def residuals(s, c, rounded, start, size):
        step = min(size, BLOCK)
        for offset in range(0, size, step):
            top = pl.multiple_of(start + offset, step)
            predicted = lax.dot_general(
                users[pl.ds(top, step), :], rounded, (((1,), (1,)), ((), ())),
                preferred_element_type=jnp.float32,
            )
            for i in range(step // TILE):
                for j in range(wide):
                    slot = slot_ref[s, (top // TILE + i) * col_tiles + c * wide + j]
                    live = (slot < slots).astype(jnp.float32)
                    rated = ratings[s][jnp.minimum(slot, slots - 1)].astype(jnp.float32)
                    guess = predicted[i * TILE : (i + 1) * TILE, j * TILE : (j + 1) * TILE]
                    residual[
                        pl.ds(pl.multiple_of(top + i * TILE, TILE), TILE),
                        j * TILE : (j + 1) * TILE,
                    ] = ((guess - rated) * live).astype(jnp.bfloat16)

    def update(s, c, panel):
        item_grad = lax.dot_general(
            residual[...], users[...], (((0,), (0,)), ((), ())),
            preferred_element_type=jnp.float32,
        )
        held[s][part(c), :] = panel - learn_rate * (item_grad + weight_decay * panel)

    def add_users(rounded, start, size):
        step = min(size, BLOCK)
        for offset in range(0, size, step):
            here = pl.ds(pl.multiple_of(start + offset, step), step)
            total[here, :] += jnp.dot(
                residual[here, :], rounded, preferred_element_type=jnp.float32
            )

    total[...] = jnp.zeros_like(total)
    map_slots.wait()
    load_users.wait()
    for s in range(steps):
        load_rates[s].wait()

        def work(c, carry, s=s):
            if s == 0:
                pltpu.make_async_copy(
                    panel_hbm.at[part(c)], held[0].at[part(c)], load_sem.at[c]
                ).wait()
            else:
                send(s - 1, c).wait_recv()
            panel = held[s][part(c), :]
            rounded = panel.astype(jnp.bfloat16)
            residuals(s, c, rounded, 0, rows)
            update(s, c, panel)
            if s < steps - 1:
                if s == 0:
                    @pl.when(c == 0)
                    def _():
                        pl.semaphore_wait(barrier, groups)

                    @pl.when(c >= FLIGHT)
                    def _():
                        send(0, c - FLIGHT).wait_send()
                else:
                    @pl.when(c >= FLIGHT)
                    def _():
                        send(s, c - FLIGHT).wait_send()

                    @pl.when(c < FLIGHT)
                    def _():
                        send(s - 1, chunks + c - FLIGHT).wait_send()
                send(s, c).start()
            else:
                write(c).start()
            add_users(rounded, 0, rows)
            return carry

        lax.fori_loop(0, chunks if s < steps - 1 else chunks - 1, work, 0)

    block = min(share, BLOCK)

    def exchange(d, b):
        peer = lax.rem(g + d, groups)
        top = pl.multiple_of(peer * share + b * block, block)
        return pltpu.make_async_remote_copy(
            src_ref=total.at[pl.ds(top, block)],
            dst_ref=grad_in.at[d - 1, pl.ds(b * block, block)],
            send_sem=grad_send.at[d - 1, b],
            recv_sem=grad_recv.at[d - 1, b],
            device_id={"item": peer},
            device_id_type=MESH,
        )

    def finish(b):
        here = pl.ds(pl.multiple_of(g * share + b * block, block), block)
        return here, pltpu.make_async_copy(
            total.at[here], grad_out.at[pl.ds(b * block, block)], grad_sem.at[b]
        )

    final, last = steps - 1, chunks - 1
    send(final - 1, last).wait_recv()
    panel = held[final][part(last), :]
    rounded = panel.astype(jnp.bfloat16)
    parts = [(d, b) for d in range(1, groups) for b in range(share // block)]
    for d, b in parts:
        top = lax.rem(g + d, groups) * share + b * block
        residuals(final, last, rounded, top, block)
        add_users(rounded, top, block)
        exchange(d, b).start()
    residuals(final, last, rounded, g * share, share)
    update(final, last, panel)
    write(last).start()
    add_users(rounded, g * share, share)
    for b in range(share // block):
        here, done = finish(b)
        for d in range(1, groups):
            exchange(d, b).wait_recv()
            total[here, :] += grad_in[d - 1, pl.ds(b * block, block), :]
        total[here, :] = user_scale * total[here, :]
        done.start()
    for d, b in parts:
        exchange(d, b).wait_send()
    for c in range(chunks - FLIGHT, chunks):
        send(final - 1, c).wait_send()
    for c in range(chunks):
        write(c).wait()
    for b in range(share // block):
        finish(b)[1].wait()


def place(held, gradient, panel_out, grad_out, panel_sem, grad_sem):
    copies = []
    for source, target, sem in ((held, panel_out, panel_sem), (gradient, grad_out, grad_sem)):
        size = source.shape[0] // PIECES
        for piece in range(PIECES):
            here = pl.ds(piece * size, size)
            copies.append(
                pltpu.make_async_copy(source.at[here], target.at[here], sem.at[piece])
            )
    for copy in copies:
        copy.start()
    for copy in copies:
        copy.wait()


def shards(user_factors, item_panels, ratings, tile_ids, tile_count):
    cycle, groups = lax.axis_size("user"), lax.axis_size("item")
    rows, rank = user_factors.shape
    items = item_panels.shape[0]
    steps, slots = ratings.shape[:2]
    chunks = items // CHUNK
    tiles = (rows // TILE) * (items // TILE)
    share = rows // groups
    blocks = share // min(share, BLOCK)

    ids = tile_ids.reshape(steps, 1, slots)
    count = tile_count.reshape(steps)

    scalars = pl.BlockSpec(memory_space=pltpu.SMEM)
    distant = pl.BlockSpec(memory_space=pltpu.HBM)
    anywhere = pl.BlockSpec(memory_space=pl.ANY)
    held, gradient = pl.pallas_call(
        functools.partial(kernel, steps, cycle, groups),
        out_shape=(
            pltpu.VMEM((items, rank), jnp.float32),
            pltpu.VMEM((share, rank), jnp.float32),
        ),
        in_specs=[scalars] * 2 + [distant] * 3,
        out_specs=(anywhere, anywhere),
        scratch_shapes=[
            pltpu.VMEM((steps, tiles), jnp.int32),
            pltpu.SMEM((steps, tiles), jnp.int32),
            pltpu.VMEM((rows, rank), jnp.bfloat16),
            pltpu.VMEM((rows, rank), jnp.float32),
            pltpu.VMEM((rows, CHUNK), jnp.bfloat16),
            pltpu.VMEM((max(groups - 1, 1), share, rank), jnp.float32),
            [pltpu.VMEM((items, rank), jnp.float32) for _ in range(steps)],
            [pltpu.VMEM((slots, TILE, TILE), jnp.bfloat16) for _ in range(steps)],
            pltpu.SemaphoreType.DMA((chunks + 1,)),
            pltpu.SemaphoreType.DMA((steps,)),
            pltpu.SemaphoreType.DMA,
            pltpu.SemaphoreType.DMA((steps - 1, chunks)),
            pltpu.SemaphoreType.DMA((steps - 1, chunks)),
            pltpu.SemaphoreType.DMA((chunks,)),
            pltpu.SemaphoreType.DMA((blocks,)),
            pltpu.SemaphoreType.DMA((max(groups - 1, 1), blocks)),
            pltpu.SemaphoreType.DMA((max(groups - 1, 1), blocks)),
        ],
        compiler_params=pltpu.CompilerParams(
            collective_id=0, has_side_effects=True, vmem_limit_bytes=56 * 2**20
        ),
        name="sub_epoch",
    )(
        ids, count,
        *(pltpu.with_memory_space_constraint(x, pltpu.HBM) for x in (user_factors, item_panels, ratings)),
    )
    return pl.pallas_call(
        place,
        out_shape=(
            jax.ShapeDtypeStruct(held.shape, held.dtype),
            jax.ShapeDtypeStruct(gradient.shape, gradient.dtype),
        ),
        in_specs=[anywhere] * 2,
        out_specs=(anywhere, anywhere),
        scratch_shapes=[pltpu.SemaphoreType.DMA((PIECES,)), pltpu.SemaphoreType.DMA((PIECES,))],
        compiler_params=pltpu.CompilerParams(vmem_limit_bytes=4 * 2**20),
        name="place",
    )(*(pltpu.with_memory_space_constraint(x, pltpu.VMEM) for x in (held, gradient)))


def solution(mesh):
    in_specs = (
        P("user", None),
        P(("user", "item"), None),
        P(None, "user", "item", None),
        P(None, "user", "item"),
        P(None, "user", "item"),
    )
    out_specs = (P(("user", "item"), None), P(("user", "item"), None))
    return jax.shard_map(shards, mesh=mesh, in_specs=in_specs, out_specs=out_specs, check_vma=False)
```

```python
import functools

import jax
import jax.numpy as jnp
from jax import lax
from jax.experimental import pallas as pl
from jax.experimental.pallas import tpu as pltpu
from jax.sharding import PartitionSpec as P

TILE = 128
CHUNK = 256
BLOCK = 256
FLIGHT = 2
PIECES = 4
MESH = pl.DeviceIdType.MESH

learn_rate = 0.05
weight_decay = 0.02
user_scale = 1.0 / 64.0


def kernel(
    steps, cycle, groups,
    ids_ref, count_ref, users_hbm, panel_hbm, ratings_hbm, panel_out, grad_out,
    slot_rows, slot_ref, users, total, residual, grad_in, held, ratings,
    load_sem, rate_sem, slot_sem, send_sem, recv_sem, out_sem, grad_sem, grad_send, grad_recv,
):
    rows, rank = users.shape
    items = held[0].shape[0]
    slots = ratings[0].shape[0]
    row_tiles, col_tiles = rows // TILE, items // TILE
    chunks = items // CHUNK
    wide = CHUNK // TILE
    share = rows // groups

    u = lax.axis_index("user")
    g = lax.axis_index("item")
    right, left = lax.rem(u + 1, cycle), lax.rem(u + cycle - 1, cycle)

    barrier = pltpu.get_barrier_semaphore()
    pl.semaphore_signal(barrier, inc=1, device_id={"user": left}, device_id_type=MESH)
    for d in range(1, groups):
        pl.semaphore_signal(
            barrier, inc=1, device_id={"item": lax.rem(g + d, groups)}, device_id_type=MESH
        )

    def part(c):
        return pl.ds(pl.multiple_of(c * CHUNK, CHUNK), CHUNK)

    load_users = pltpu.make_async_copy(users_hbm, users, load_sem.at[chunks])
    load_panel = [
        pltpu.make_async_copy(panel_hbm.at[part(c)], held[0].at[part(c)], load_sem.at[c])
        for c in range(chunks)
    ]
    load_rates = [
        pltpu.make_async_copy(ratings_hbm.at[s], ratings[s], rate_sem.at[s]) for s in range(steps)
    ]
    load_panel[0].start()
    load_users.start()
    load_rates[0].start()
    for c in range(1, chunks):
        load_panel[c].start()
    for s in range(1, steps):
        load_rates[s].start()

    def send(s, c):
        return pltpu.make_async_remote_copy(
            src_ref=held[s].at[part(c)],
            dst_ref=held[s + 1].at[part(c)],
            send_sem=send_sem.at[s, c],
            recv_sem=recv_sem.at[s, c],
            device_id={"user": right},
            device_id_type=MESH,
        )

    def write(c):
        return pltpu.make_async_copy(held[-1].at[part(c)], panel_out.at[part(c)], out_sem.at[c])

    tile = lax.broadcasted_iota(jnp.int32, (1, slot_rows.shape[1]), 1)
    for s in range(steps):
        slot_of = jnp.full(tile.shape, slots, jnp.int32)
        for k in range(slots):
            listed = jnp.where(k < count_ref[s], ids_ref[s, 0, k], -1)
            slot_of = jnp.where(tile == listed, k, slot_of)
        slot_rows[s : s + 1, :] = slot_of
    map_slots = pltpu.make_async_copy(slot_rows, slot_ref, slot_sem)
    map_slots.start()

    def residuals(s, c, rounded, start, size):
        step = min(size, BLOCK)
        for offset in range(0, size, step):
            top = pl.multiple_of(start + offset, step)
            predicted = lax.dot_general(
                users[pl.ds(top, step), :], rounded, (((1,), (1,)), ((), ())),
                preferred_element_type=jnp.float32,
            )
            for i in range(step // TILE):
                for j in range(wide):
                    slot = slot_ref[s, (top // TILE + i) * col_tiles + c * wide + j]
                    live = (slot < slots).astype(jnp.float32)
                    rated = ratings[s][jnp.minimum(slot, slots - 1)].astype(jnp.float32)
                    guess = predicted[i * TILE : (i + 1) * TILE, j * TILE : (j + 1) * TILE]
                    residual[
                        pl.ds(pl.multiple_of(top + i * TILE, TILE), TILE),
                        j * TILE : (j + 1) * TILE,
                    ] = ((guess - rated) * live).astype(jnp.bfloat16)

    def update(s, c, panel):
        item_grad = lax.dot_general(
            residual[...], users[...], (((0,), (0,)), ((), ())),
            preferred_element_type=jnp.float32,
        )
        held[s][part(c), :] = panel - learn_rate * (item_grad + weight_decay * panel)

    def add_users(rounded, start, size):
        step = min(size, BLOCK)
        for offset in range(0, size, step):
            here = pl.ds(pl.multiple_of(start + offset, step), step)
            total[here, :] += jnp.dot(
                residual[here, :], rounded, preferred_element_type=jnp.float32
            )

    total[...] = jnp.zeros_like(total)
    map_slots.wait()
    load_users.wait()
    for s in range(steps):
        load_rates[s].wait()

        def work(c, carry, s=s):
            if s == 0:
                pltpu.make_async_copy(
                    panel_hbm.at[part(c)], held[0].at[part(c)], load_sem.at[c]
                ).wait()
            else:
                send(s - 1, c).wait_recv()
            panel = held[s][part(c), :]
            rounded = panel.astype(jnp.bfloat16)
            residuals(s, c, rounded, 0, rows)
            update(s, c, panel)
            if s < steps - 1:
                if s == 0:
                    @pl.when(c == 0)
                    def _():
                        pl.semaphore_wait(barrier, groups)

                    @pl.when(c >= FLIGHT)
                    def _():
                        send(0, c - FLIGHT).wait_send()
                else:
                    @pl.when(c >= FLIGHT)
                    def _():
                        send(s, c - FLIGHT).wait_send()

                    @pl.when(c < FLIGHT)
                    def _():
                        send(s - 1, chunks + c - FLIGHT).wait_send()
                send(s, c).start()
            else:
                write(c).start()
            add_users(rounded, 0, rows)
            return carry

        lax.fori_loop(0, chunks if s < steps - 1 else chunks - 1, work, 0)

    block = min(share, BLOCK)

    def exchange(d, b):
        peer = lax.rem(g + d, groups)
        top = pl.multiple_of(peer * share + b * block, block)
        return pltpu.make_async_remote_copy(
            src_ref=total.at[pl.ds(top, block)],
            dst_ref=grad_in.at[d - 1, pl.ds(b * block, block)],
            send_sem=grad_send.at[d - 1, b],
            recv_sem=grad_recv.at[d - 1, b],
            device_id={"item": peer},
            device_id_type=MESH,
        )

    def finish(b):
        here = pl.ds(pl.multiple_of(g * share + b * block, block), block)
        return here, pltpu.make_async_copy(
            total.at[here], grad_out.at[pl.ds(b * block, block)], grad_sem.at[b]
        )

    final, last = steps - 1, chunks - 1
    send(final - 1, last).wait_recv()
    panel = held[final][part(last), :]
    rounded = panel.astype(jnp.bfloat16)
    parts = [(d, b) for d in range(1, groups) for b in range(share // block)]
    for d, b in parts:
        top = lax.rem(g + d, groups) * share + b * block
        residuals(final, last, rounded, top, block)
        add_users(rounded, top, block)
        exchange(d, b).start()
    residuals(final, last, rounded, g * share, share)
    update(final, last, panel)
    write(last).start()
    add_users(rounded, g * share, share)
    for b in range(share // block):
        here, done = finish(b)
        for d in range(1, groups):
            exchange(d, b).wait_recv()
            total[here, :] += grad_in[d - 1, pl.ds(b * block, block), :]
        total[here, :] = user_scale * total[here, :]
        done.start()
    for d, b in parts:
        exchange(d, b).wait_send()
    for c in range(chunks - FLIGHT, chunks):
        send(final - 1, c).wait_send()
    for c in range(chunks):
        write(c).wait()
    for b in range(share // block):
        finish(b)[1].wait()


def place(held, gradient, panel_out, grad_out, panel_sem, grad_sem):
    copies = []
    for source, target, sem in ((held, panel_out, panel_sem), (gradient, grad_out, grad_sem)):
        size = source.shape[0] // PIECES
        for piece in range(PIECES):
            here = pl.ds(piece * size, size)
            copies.append(
                pltpu.make_async_copy(source.at[here], target.at[here], sem.at[piece])
            )
    for copy in copies:
        copy.start()
    for copy in copies:
        copy.wait()


def shards(user_factors, item_panels, ratings, tile_ids, tile_count):
    cycle, groups = lax.axis_size("user"), lax.axis_size("item")
    rows, rank = user_factors.shape
    items = item_panels.shape[0]
    steps, slots = ratings.shape[:2]
    chunks = items // CHUNK
    tiles = (rows // TILE) * (items // TILE)
    share = rows // groups
    blocks = share // min(share, BLOCK)

    ids = tile_ids.reshape(steps, 1, slots)
    count = tile_count.reshape(steps)

    scalars = pl.BlockSpec(memory_space=pltpu.SMEM)
    distant = pl.BlockSpec(memory_space=pltpu.HBM)
    anywhere = pl.BlockSpec(memory_space=pl.ANY)
    held, gradient = pl.pallas_call(
        functools.partial(kernel, steps, cycle, groups),
        out_shape=(
            pltpu.VMEM((items, rank), jnp.float32),
            pltpu.VMEM((share, rank), jnp.float32),
        ),
        in_specs=[scalars] * 2 + [distant] * 3,
        out_specs=(anywhere, anywhere),
        scratch_shapes=[
            pltpu.VMEM((steps, tiles), jnp.int32),
            pltpu.SMEM((steps, tiles), jnp.int32),
            pltpu.VMEM((rows, rank), jnp.bfloat16),
            pltpu.VMEM((rows, rank), jnp.float32),
            pltpu.VMEM((rows, CHUNK), jnp.bfloat16),
            pltpu.VMEM((max(groups - 1, 1), share, rank), jnp.float32),
            [pltpu.VMEM((items, rank), jnp.float32) for _ in range(steps)],
            [pltpu.VMEM((slots, TILE, TILE), jnp.bfloat16) for _ in range(steps)],
            pltpu.SemaphoreType.DMA((chunks + 1,)),
            pltpu.SemaphoreType.DMA((steps,)),
            pltpu.SemaphoreType.DMA,
            pltpu.SemaphoreType.DMA((steps - 1, chunks)),
            pltpu.SemaphoreType.DMA((steps - 1, chunks)),
            pltpu.SemaphoreType.DMA((chunks,)),
            pltpu.SemaphoreType.DMA((blocks,)),
            pltpu.SemaphoreType.DMA((max(groups - 1, 1), blocks)),
            pltpu.SemaphoreType.DMA((max(groups - 1, 1), blocks)),
        ],
        compiler_params=pltpu.CompilerParams(
            collective_id=0, has_side_effects=True, vmem_limit_bytes=56 * 2**20
        ),
        name="sub_epoch",
    )(
        ids, count,
        *(pltpu.with_memory_space_constraint(x, pltpu.HBM) for x in (user_factors, item_panels, ratings)),
    )
    return pl.pallas_call(
        place,
        out_shape=(
            jax.ShapeDtypeStruct(held.shape, held.dtype),
            jax.ShapeDtypeStruct(gradient.shape, gradient.dtype),
        ),
        in_specs=[anywhere] * 2,
        out_specs=(anywhere, anywhere),
        scratch_shapes=[pltpu.SemaphoreType.DMA((PIECES,)), pltpu.SemaphoreType.DMA((PIECES,))],
        compiler_params=pltpu.CompilerParams(vmem_limit_bytes=4 * 2**20),
        name="place",
    )(*(pltpu.with_memory_space_constraint(x, pltpu.VMEM) for x in (held, gradient)))


def solution(mesh):
    in_specs = (
        P("user", None),
        P(("user", "item"), None),
        P(None, "user", "item", None),
        P(None, "user", "item"),
        P(None, "user", "item"),
    )
    out_specs = (P(("user", "item"), None), P(("user", "item"), None))
    return jax.shard_map(shards, mesh=mesh, in_specs=in_specs, out_specs=out_specs, check_vma=False)
```

```python
import functools

import jax
import jax.numpy as jnp
from jax import lax
from jax.experimental import pallas as pl
from jax.experimental.pallas import tpu as pltpu
from jax.sharding import PartitionSpec as P

TILE = 128
CHUNK = 256
BLOCK = 256
FLIGHT = 2
PIECES = 4
MESH = pl.DeviceIdType.MESH

learn_rate = 0.05
weight_decay = 0.02
user_scale = 1.0 / 64.0


def kernel(
    steps, cycle, groups,
    ids_ref, count_ref, users_hbm, panel_hbm, ratings_hbm, panel_out, grad_out,
    slot_rows, slot_ref, users, total, residual, grad_in, held, ratings,
    load_sem, rate_sem, slot_sem, send_sem, recv_sem, out_sem, grad_sem, grad_send, grad_recv,
):
    rows, rank = users.shape
    items = held[0].shape[0]
    slots = ratings[0].shape[0]
    row_tiles, col_tiles = rows // TILE, items // TILE
    chunks = items // CHUNK
    wide = CHUNK // TILE
    share = rows // groups

    u = lax.axis_index("user")
    g = lax.axis_index("item")
    right, left = lax.rem(u + 1, cycle), lax.rem(u + cycle - 1, cycle)

    barrier = pltpu.get_barrier_semaphore()
    pl.semaphore_signal(barrier, inc=1, device_id={"user": left}, device_id_type=MESH)
    for d in range(1, groups):
        pl.semaphore_signal(
            barrier, inc=1, device_id={"item": lax.rem(g + d, groups)}, device_id_type=MESH
        )

    def part(c):
        return pl.ds(pl.multiple_of(c * CHUNK, CHUNK), CHUNK)

    load_users = pltpu.make_async_copy(users_hbm, users, load_sem.at[chunks])
    load_panel = [
        pltpu.make_async_copy(panel_hbm.at[part(c)], held[0].at[part(c)], load_sem.at[c])
        for c in range(chunks)
    ]
    load_rates = [
        pltpu.make_async_copy(ratings_hbm.at[s], ratings[s], rate_sem.at[s]) for s in range(steps)
    ]
    load_panel[0].start()
    load_users.start()
    load_rates[0].start()

    def send(s, c):
        return pltpu.make_async_remote_copy(
            src_ref=held[s].at[part(c)],
            dst_ref=held[s + 1].at[part(c)],
            send_sem=send_sem.at[s, c],
            recv_sem=recv_sem.at[s, c],
            device_id={"user": right},
            device_id_type=MESH,
        )

    def write(c):
        return pltpu.make_async_copy(held[-1].at[part(c)], panel_out.at[part(c)], out_sem.at[c])

    tile = lax.broadcasted_iota(jnp.int32, (1, slot_rows.shape[1]), 1)
    for s in range(steps):
        slot_of = jnp.full(tile.shape, slots, jnp.int32)
        for k in range(slots):
            listed = jnp.where(k < count_ref[s], ids_ref[s, 0, k], -1)
            slot_of = jnp.where(tile == listed, k, slot_of)
        slot_rows[s : s + 1, :] = slot_of
    map_slots = pltpu.make_async_copy(slot_rows, slot_ref, slot_sem)
    map_slots.start()

    def residuals(s, c, rounded, start, size):
        step = min(size, BLOCK)
        for offset in range(0, size, step):
            top = pl.multiple_of(start + offset, step)
            predicted = lax.dot_general(
                users[pl.ds(top, step), :], rounded, (((1,), (1,)), ((), ())),
                preferred_element_type=jnp.float32,
            )
            for i in range(step // TILE):
                for j in range(wide):
                    slot = slot_ref[s, (top // TILE + i) * col_tiles + c * wide + j]
                    live = (slot < slots).astype(jnp.float32)
                    rated = ratings[s][jnp.minimum(slot, slots - 1)].astype(jnp.float32)
                    guess = predicted[i * TILE : (i + 1) * TILE, j * TILE : (j + 1) * TILE]
                    residual[
                        pl.ds(pl.multiple_of(top + i * TILE, TILE), TILE),
                        j * TILE : (j + 1) * TILE,
                    ] = ((guess - rated) * live).astype(jnp.bfloat16)

    def update(s, c, panel):
        item_grad = lax.dot_general(
            residual[...], users[...], (((0,), (0,)), ((), ())),
            preferred_element_type=jnp.float32,
        )
        held[s][part(c), :] = panel - learn_rate * (item_grad + weight_decay * panel)

    def add_users(rounded, start, size):
        step = min(size, BLOCK)
        for offset in range(0, size, step):
            here = pl.ds(pl.multiple_of(start + offset, step), step)
            total[here, :] += jnp.dot(
                residual[here, :], rounded, preferred_element_type=jnp.float32
            )

    total[...] = jnp.zeros_like(total)
    map_slots.wait()
    load_users.wait()
    for s in range(steps):
        load_rates[s].wait()
        if s == 0:
            for c in range(1, chunks):
                load_panel[c].start()
        if s < steps - 1:
            load_rates[s + 1].start()

        def work(c, carry, s=s):
            if s == 0:
                pltpu.make_async_copy(
                    panel_hbm.at[part(c)], held[0].at[part(c)], load_sem.at[c]
                ).wait()
            else:
                send(s - 1, c).wait_recv()
            panel = held[s][part(c), :]
            rounded = panel.astype(jnp.bfloat16)
            residuals(s, c, rounded, 0, rows)
            update(s, c, panel)
            if s < steps - 1:
                if s == 0:
                    @pl.when(c == 0)
                    def _():
                        pl.semaphore_wait(barrier, groups)

                    @pl.when(c >= FLIGHT)
                    def _():
                        send(0, c - FLIGHT).wait_send()
                else:
                    @pl.when(c >= FLIGHT)
                    def _():
                        send(s, c - FLIGHT).wait_send()

                    @pl.when(c < FLIGHT)
                    def _():
                        send(s - 1, chunks + c - FLIGHT).wait_send()
                send(s, c).start()
            else:
                write(c).start()
            add_users(rounded, 0, rows)
            return carry

        lax.fori_loop(0, chunks if s < steps - 1 else chunks - 1, work, 0)

    block = min(share, BLOCK)

    def exchange(d, b):
        peer = lax.rem(g + d, groups)
        top = pl.multiple_of(peer * share + b * block, block)
        return pltpu.make_async_remote_copy(
            src_ref=total.at[pl.ds(top, block)],
            dst_ref=grad_in.at[d - 1, pl.ds(b * block, block)],
            send_sem=grad_send.at[d - 1, b],
            recv_sem=grad_recv.at[d - 1, b],
            device_id={"item": peer},
            device_id_type=MESH,
        )

    def finish(b):
        here = pl.ds(pl.multiple_of(g * share + b * block, block), block)
        return here, pltpu.make_async_copy(
            total.at[here], grad_out.at[pl.ds(b * block, block)], grad_sem.at[b]
        )

    final, last = steps - 1, chunks - 1
    send(final - 1, last).wait_recv()
    panel = held[final][part(last), :]
    rounded = panel.astype(jnp.bfloat16)
    parts = [(d, b) for d in range(1, groups) for b in range(share // block)]
    for d, b in parts:
        top = lax.rem(g + d, groups) * share + b * block
        residuals(final, last, rounded, top, block)
        add_users(rounded, top, block)
        exchange(d, b).start()
    residuals(final, last, rounded, g * share, share)
    update(final, last, panel)
    write(last).start()
    add_users(rounded, g * share, share)
    for b in range(share // block):
        here, done = finish(b)
        for d in range(1, groups):
            exchange(d, b).wait_recv()
            total[here, :] += grad_in[d - 1, pl.ds(b * block, block), :]
        total[here, :] = user_scale * total[here, :]
        done.start()
    for d, b in parts:
        exchange(d, b).wait_send()
    for c in range(chunks - FLIGHT, chunks):
        send(final - 1, c).wait_send()
    for c in range(chunks):
        write(c).wait()
    for b in range(share // block):
        finish(b)[1].wait()


def place(held, gradient, panel_out, grad_out, panel_sem, grad_sem):
    copies = []
    for source, target, sem in ((held, panel_out, panel_sem), (gradient, grad_out, grad_sem)):
        size = source.shape[0] // PIECES
        for piece in range(PIECES):
            here = pl.ds(piece * size, size)
            copies.append(
                pltpu.make_async_copy(source.at[here], target.at[here], sem.at[piece])
            )
    for copy in copies:
        copy.start()
    for copy in copies:
        copy.wait()


def shards(user_factors, item_panels, ratings, tile_ids, tile_count):
    cycle, groups = lax.axis_size("user"), lax.axis_size("item")
    rows, rank = user_factors.shape
    items = item_panels.shape[0]
    steps, slots = ratings.shape[:2]
    chunks = items // CHUNK
    tiles = (rows // TILE) * (items // TILE)
    share = rows // groups
    blocks = share // min(share, BLOCK)

    ids = tile_ids.reshape(steps, 1, slots)
    count = tile_count.reshape(steps)

    scalars = pl.BlockSpec(memory_space=pltpu.SMEM)
    distant = pl.BlockSpec(memory_space=pltpu.HBM)
    anywhere = pl.BlockSpec(memory_space=pl.ANY)
    held, gradient = pl.pallas_call(
        functools.partial(kernel, steps, cycle, groups),
        out_shape=(
            pltpu.VMEM((items, rank), jnp.float32),
            pltpu.VMEM((share, rank), jnp.float32),
        ),
        in_specs=[scalars] * 2 + [distant] * 3,
        out_specs=(anywhere, anywhere),
        scratch_shapes=[
            pltpu.VMEM((steps, tiles), jnp.int32),
            pltpu.SMEM((steps, tiles), jnp.int32),
            pltpu.VMEM((rows, rank), jnp.bfloat16),
            pltpu.VMEM((rows, rank), jnp.float32),
            pltpu.VMEM((rows, CHUNK), jnp.bfloat16),
            pltpu.VMEM((max(groups - 1, 1), share, rank), jnp.float32),
            [pltpu.VMEM((items, rank), jnp.float32) for _ in range(steps)],
            [pltpu.VMEM((slots, TILE, TILE), jnp.bfloat16) for _ in range(steps)],
            pltpu.SemaphoreType.DMA((chunks + 1,)),
            pltpu.SemaphoreType.DMA((steps,)),
            pltpu.SemaphoreType.DMA,
            pltpu.SemaphoreType.DMA((steps - 1, chunks)),
            pltpu.SemaphoreType.DMA((steps - 1, chunks)),
            pltpu.SemaphoreType.DMA((chunks,)),
            pltpu.SemaphoreType.DMA((blocks,)),
            pltpu.SemaphoreType.DMA((max(groups - 1, 1), blocks)),
            pltpu.SemaphoreType.DMA((max(groups - 1, 1), blocks)),
        ],
        compiler_params=pltpu.CompilerParams(
            collective_id=0, has_side_effects=True, vmem_limit_bytes=56 * 2**20
        ),
        name="sub_epoch",
    )(
        ids, count,
        *(pltpu.with_memory_space_constraint(x, pltpu.HBM) for x in (user_factors, item_panels, ratings)),
    )
    return pl.pallas_call(
        place,
        out_shape=(
            jax.ShapeDtypeStruct(held.shape, held.dtype),
            jax.ShapeDtypeStruct(gradient.shape, gradient.dtype),
        ),
        in_specs=[anywhere] * 2,
        out_specs=(anywhere, anywhere),
        scratch_shapes=[pltpu.SemaphoreType.DMA((PIECES,)), pltpu.SemaphoreType.DMA((PIECES,))],
        compiler_params=pltpu.CompilerParams(vmem_limit_bytes=4 * 2**20),
        name="place",
    )(*(pltpu.with_memory_space_constraint(x, pltpu.VMEM) for x in (held, gradient)))


def solution(mesh):
    in_specs = (
        P("user", None),
        P(("user", "item"), None),
        P(None, "user", "item", None),
        P(None, "user", "item"),
        P(None, "user", "item"),
    )
    out_specs = (P(("user", "item"), None), P(("user", "item"), None))
    return jax.shard_map(shards, mesh=mesh, in_specs=in_specs, out_specs=out_specs, check_vma=False)
```
